512 devices in a mesh: dp: 16 (over x, y), fsdp: 32 (over z, core).
Axes of the slice: x: 4, y: 4, z: 16, core: 2. Of those that a mesh axis runs over, the one named last changes fastest.
Arguments:
- owners: int32 [576], P('dp'), parts along dimension 0, may hold values from 0 to 31, as said below
- grads: bfloat16 [64, 512, 4608], P('dp', 'fsdp'), parts along dimension 0, may hold values from -1.1953125 to 1.1953125
- roots: bfloat16 [1024, 2, 512, 512], P(('dp', 'fsdp')), parts along dimension 0, may hold values from -1 to 3, as said below
Outputs:
- direction: bfloat16 [64, 512, 4608], P('dp', 'fsdp'), parts along dimension 0
- grams: bfloat16 [1024, 2, 512, 512], P(('dp', 'fsdp')), parts along dimension 0
The draws below stay inside these ranges and needn't reach their ends.
There are 16 independent parts, one for each index of `dp`. The reference program is written for one: setup_inputs(seed, part) draws one part's arguments, and reference() takes and returns one part's arrays. A program takes and returns all parts, laid end to end along the dimension named above; each array names one. Nothing has to cross between parts.
Inputs may be any that keep to these rules, and one draw needn't show every extreme that they name: `owners`: no device is assigned more than 2 blocks, and some device exactly 2. `roots`: each factor is symmetric.
All inputs are finite; a program needn't handle non-finite values.
Results may differ from the reference program's by a relative error of at most 0.0049.
Values may be sent and summed in bfloat16 or wider, within the bound.
A program may use at most 128 MiB of HBM per device.

```python
import jax
import jax.numpy as jnp

B = 512
COLS = 4608
MOST = 2
SLABS = 4
NCOL = 9
BLOCKS = 36
N_FSDP = 32


def draw_owners(key, part):
    key = jax.random.fold_in(key, 11)
    first_key, second_key, third_key = jax.random.split(key, 3)
    total_slots = N_FSDP * MOST
    chosen = jax.random.randint(first_key, (), 0, N_FSDP)
    shuffled = jax.random.permutation(second_key, total_slots)
    slot_ids = jnp.arange(total_slots, dtype=jnp.int32)
    scores = jnp.where(slot_ids // MOST == chosen, 0, total_slots) + shuffled
    ranked = jnp.argsort(scores, stable=True).astype(jnp.int32)
    block_order = jax.random.permutation(third_key, BLOCKS)
    slots = jnp.zeros((BLOCKS,), jnp.int32).at[block_order].set(ranked[:BLOCKS])
    return (slots // MOST).astype(jnp.int32)


def draw_roots(key, part):
    key = jax.random.fold_in(key, 23)
    noise_key, diag_key = jax.random.split(key)
    shape = (N_FSDP * MOST, 2, B, B)
    noise = jnp.clip(jax.random.normal(noise_key, shape, jnp.float32), -4.0, 4.0)
    symmetric = (noise + jnp.swapaxes(noise, -1, -2)) * (0.5 / (2.0 * B) ** 0.5)
    diagonal = jnp.exp(jax.random.uniform(diag_key, shape[:-1], jnp.float32, -0.6931, 0.6931))
    identity = jnp.eye(B, dtype=jnp.float32)
    return (symmetric + identity * diagonal[..., None]).astype(jnp.bfloat16)


def block_scale(stream_key, extent, shards, low, largest):
    def one(dim, shards_of):
        draws = jax.random.uniform(jax.random.fold_in(jax.random.fold_in(stream_key, 6), dim), (shards_of,), jnp.float32, low / len(shards), largest / len(shards))
        return jnp.repeat(jnp.exp(draws), extent[dim] // shards_of).reshape((-1,) + (1,) * (len(extent) - dim - 1))

    gain = one(*shards[0])
    for cut in shards[1:]:
        gain = gain * one(*cut)
    return gain


def scatter_about(own_key, dims, scale, limit, shards=(), held_as=jnp.bfloat16):
    level = block_scale(own_key, dims, shards, -0.22, 0.18) if shards else 1.0
    values = jax.random.normal(own_key, dims, jnp.float32) * scale * level
    return jnp.minimum(jnp.maximum(values, -limit), limit).astype(held_as)


def setup_inputs(seed: int = 0, part: int = 0) -> dict:
    seeds = jax.random.split(jax.random.key(seed), 4)
    part_keys = jax.random.split(jax.random.fold_in(seeds[3], part), 4)
    return {
        "owners": draw_owners(jax.random.fold_in(jax.random.fold_in(seeds[3], part), 71), part),
        "grads": scatter_about(part_keys[1], (SLABS, B, COLS), 0.2, 1.1953125, ((1, 32),)),
        "roots": draw_roots(jax.random.fold_in(jax.random.fold_in(seeds[3], part), 71), part),
    }


def reference(owners, grads, roots):
    position = jnp.arange(BLOCKS, dtype=jnp.int32)
    same_owner = owners[:, None] == owners[None, :]
    order_within = jnp.sum(same_owner & (position[None, :] < position[:, None]), axis=1).astype(jnp.int32)
    slot_index = (owners * MOST + order_within).astype(jnp.int32)
    gram_pairs = jnp.zeros((N_FSDP * MOST, 2, B, B), jnp.bfloat16)
    slab_list = []
    for slab_number in range(SLABS):
        pieces = []
        for column_block in range(NCOL):
            number = slab_number * NCOL + column_block
            tile_block = grads[slab_number, :, column_block * B:(column_block + 1) * B]
            left_root = roots[slot_index[number], 0]
            right_root = roots[slot_index[number], 1]
            gram_left = jnp.dot(tile_block, tile_block.T, preferred_element_type=jnp.float32).astype(jnp.bfloat16)
            gram_right = jnp.dot(tile_block.T, tile_block, preferred_element_type=jnp.float32).astype(jnp.bfloat16)
            gram_pairs = gram_pairs.at[slot_index[number]].set(jnp.stack([gram_left, gram_right]))
            product = jnp.dot(tile_block, right_root, preferred_element_type=jnp.float32).astype(jnp.bfloat16)
            pieces.append(jnp.dot(left_root, product, preferred_element_type=jnp.float32).astype(jnp.bfloat16))
        slab_list.append(jnp.concatenate(pieces, axis=1))
    return jnp.stack(slab_list), gram_pairs
```

```python
import functools

import jax
import jax.numpy as jnp
from jax import lax
from jax.experimental import pallas as pl
from jax.experimental.pallas import tpu as pltpu
from jax.sharding import PartitionSpec as P

MESH = pl.DeviceIdType.MESH


def offsets(chips):
    order = [(0, 1)]
    for distance in range(1, chips // 2 + 1):
        for step in sorted({distance, chips - distance}):
            order += [(step, 0), (step, 1)]
    return order


def kernel(
    sizes, owners_ref, grads_ref, roots_ref, dir_ref, grams_ref,
    gv, packed, blocks, roots_v, outgoing, returned, dir_v, grams_v, table_v, table,
    load_sem, table_sem, roots_sem, send_sem, recv_sem, out_sem,
):
    devices, slabs, ncol, rows, order, slots = sizes
    total = slabs * ncol
    chips = devices // 2
    me = lax.axis_index("fsdp")
    z, core = me // 2, lax.rem(me, 2)
    partners = offsets(chips)

    def device(step, other):
        return lax.rem(z + step, chips) * 2 + lax.rem(core + other, 2)

    barrier = pltpu.get_barrier_semaphore()
    for step, other in partners:
        pl.semaphore_signal(
            barrier, inc=1, device_id={"fsdp": device(step, other)}, device_id_type=MESH
        )

    loads = []
    for k in range(total):
        s, j = divmod(k, ncol)
        loads.append(
            pltpu.make_async_copy(
                grads_ref.at[s, :, pl.ds(j * order, order)], gv.at[k], load_sem.at[k]
            )
        )
    for copy in loads:
        copy.start()
    roots_copy = pltpu.make_async_copy(roots_ref, roots_v, roots_sem)
    roots_copy.start()

    lane = lax.broadcasted_iota(jnp.int32, (8, 128), 1)
    first = jnp.full((8, 128), -1, jnp.int32)
    last = jnp.full((8, 128), -1, jnp.int32)
    for k in range(total):
        last = jnp.where(lane == owners_ref[k], k, last)
        first = jnp.where(lane == owners_ref[total - 1 - k], total - 1 - k, first)
    table_v[0] = first
    table_v[1] = jnp.where(first == last, -1, last)
    table_copy = pltpu.make_async_copy(table_v, table, table_sem)
    table_copy.start()
    table_copy.wait()
    for copy in loads:
        copy.wait()

    def pack(d, carry):
        for m in range(slots):
            packed[m, d] = gv[jnp.maximum(table[m, 0, d], 0)]
        return carry

    lax.fori_loop(0, devices, pack, 0)
    pl.semaphore_wait(barrier, len(partners))

    mine = pl.ds(pl.multiple_of(me * rows, rows), rows)
    for m in range(slots):
        pltpu.make_async_copy(
            packed.at[m, me], blocks.at[m, mine, :], recv_sem.at[0, m]
        ).start()
        for step, other in partners:
            to = device(step, other)
            pltpu.make_async_remote_copy(
                src_ref=packed.at[m, to],
                dst_ref=blocks.at[m, mine, :],
                send_sem=send_sem.at[0, m],
                recv_sem=recv_sem.at[0, m],
                device_id={"fsdp": to},
                device_id_type=MESH,
            ).start()

    roots_copy.wait()
    for m in range(slots):
        pltpu.make_async_copy(blocks.at[m], blocks.at[m], recv_sem.at[0, m]).wait()
        block = blocks[m]
        product = jnp.dot(
            block, roots_v[m, 1], preferred_element_type=jnp.float32
        ).astype(jnp.bfloat16)
        outgoing[m] = jnp.dot(
            roots_v[m, 0], product, preferred_element_type=jnp.float32
        ).astype(jnp.bfloat16)
        pltpu.make_async_copy(
            outgoing.at[m, mine, :], returned.at[m, me], recv_sem.at[1, m]
        ).start()
        for step, other in partners:
            to = device(step, other)
            pltpu.make_async_remote_copy(
                src_ref=outgoing.at[m, pl.ds(pl.multiple_of(to * rows, rows), rows), :],
                dst_ref=returned.at[m, me],
                send_sem=send_sem.at[1, m],
                recv_sem=recv_sem.at[1, m],
                device_id={"fsdp": to},
                device_id_type=MESH,
            ).start()
        kept = jnp.where(table[m, 0, me] >= 0, block, jnp.zeros_like(block))
        grams_v[m, 0] = lax.dot_general(
            kept, kept, (((1,), (1,)), ((), ())), preferred_element_type=jnp.float32
        ).astype(jnp.bfloat16)
        grams_v[m, 1] = lax.dot_general(
            kept, kept, (((0,), (0,)), ((), ())), preferred_element_type=jnp.float32
        ).astype(jnp.bfloat16)
        pltpu.make_async_copy(grams_v.at[m], grams_ref.at[m], out_sem.at[m]).start()

    for m in range(slots):
        pltpu.make_async_copy(
            returned.at[m], returned.at[m], recv_sem.at[1, m]
        ).wait()
    for k in range(total):
        s, j = divmod(k, ncol)
        owner = owners_ref[k]
        slot = jnp.where(table[0, 0, owner] == k, 0, 1)
        dir_v[s, :, j * order : (j + 1) * order] = returned[slot, owner]
    dir_copy = pltpu.make_async_copy(dir_v, dir_ref, out_sem.at[slots])
    dir_copy.start()
    dir_copy.wait()
    others = pl.ds(0, devices - 1)
    for m in range(slots):
        pltpu.make_async_copy(grams_v.at[m], grams_ref.at[m], out_sem.at[m]).wait()
        for phase in range(2):
            pltpu.make_async_copy(
                packed.at[m, others], packed.at[m, others], send_sem.at[phase, m]
            ).wait()


def local(owners, grads, roots):
    devices = lax.axis_size("fsdp")
    slabs, rows, columns = grads.shape
    slots, _, order, _ = roots.shape
    ncol = columns // order
    sizes = (devices, slabs, ncol, rows, order, slots)
    any_spec = pl.BlockSpec(memory_space=pl.ANY)
    bf16 = jnp.bfloat16
    return pl.pallas_call(
        functools.partial(kernel, sizes),
        out_shape=(
            jax.ShapeDtypeStruct(grads.shape, bf16),
            jax.ShapeDtypeStruct(roots.shape, bf16),
        ),
        in_specs=[pl.BlockSpec(memory_space=pltpu.SMEM), any_spec, any_spec],
        out_specs=(any_spec, any_spec),
        scratch_shapes=[
            pltpu.VMEM((slabs * ncol, rows, order), bf16),
            pltpu.VMEM((slots, devices, rows, order), bf16),
            pltpu.VMEM((slots, order, order), bf16),
            pltpu.VMEM(roots.shape, bf16),
            pltpu.VMEM((slots, order, order), bf16),
            pltpu.VMEM((slots, devices, rows, order), bf16),
            pltpu.VMEM(grads.shape, bf16),
            pltpu.VMEM(roots.shape, bf16),
            pltpu.VMEM((2, 8, 128), jnp.int32),
            pltpu.SMEM((2, 8, 128), jnp.int32),
            pltpu.SemaphoreType.DMA((slabs * ncol,)),
            pltpu.SemaphoreType.DMA,
            pltpu.SemaphoreType.DMA,
            pltpu.SemaphoreType.DMA((2, slots)),
            pltpu.SemaphoreType.DMA((2, slots)),
            pltpu.SemaphoreType.DMA((slots + 1,)),
        ],
        compiler_params=pltpu.CompilerParams(
            collective_id=0, has_side_effects=True, vmem_limit_bytes=32 << 20
        ),
        cost_estimate=pl.CostEstimate(
            flops=slots * 4 * 2 * order**3, bytes_accessed=6 << 20, transcendentals=0
        ),
    )(owners, grads, roots)


def solution(mesh):
    return jax.shard_map(
        local,
        mesh=mesh,
        in_specs=(P("dp"), P("dp", "fsdp", None), P(("dp", "fsdp"), None, None, None)),
        out_specs=(P("dp", "fsdp", None), P(("dp", "fsdp"), None, None, None)),
        check_vma=False,
    )
```

```python
import functools

import jax
import jax.numpy as jnp
from jax import lax
from jax.experimental import pallas as pl
from jax.experimental.pallas import tpu as pltpu
from jax.sharding import PartitionSpec as P

MESH = pl.DeviceIdType.MESH


def rings(chips):
    groups, near, far = [], 0, 1
    while near < chips // 2:
        group = [(0, 1)] if near == 0 else []
        for distance in range(near + 1, min(far, chips // 2) + 1):
            for step in sorted({distance, chips - distance}):
                group += [(step, 0), (step, 1)]
        groups.append(group)
        near, far = far, 2 * far
    return groups


def exchange(
    sizes, owners_ref, grads_ref, roots_ref, dir_v, grams_v,
    gv, packed, blocks, roots_v, outgoing, returned, table_v, table, owners,
    load_sem, table_sem, roots_sem, near_sem, send_sem, recv_sem,
):
    devices, slabs, ncol, rows, order, slots = sizes
    total = slabs * ncol
    chips = devices // 2
    me = lax.axis_index("fsdp")
    z, core = me // 2, lax.rem(me, 2)
    groups = rings(chips)

    def device(step, other):
        return lax.rem(z + step, chips) * 2 + lax.rem(core + other, 2)

    def signal(semaphore, to):
        pl.semaphore_signal(
            semaphore, inc=1, device_id={"fsdp": to}, device_id_type=MESH
        )

    barrier = pltpu.get_barrier_semaphore()
    for step, other in groups[0]:
        signal(barrier, device(step, other))

    owners_copy = pltpu.make_async_copy(owners_ref, owners, table_sem)
    owners_copy.start()
    loads = []
    for k in range(total):
        s, j = divmod(k, ncol)
        loads.append(
            pltpu.make_async_copy(
                grads_ref.at[s, :, pl.ds(j * order, order)], gv.at[k], load_sem.at[k]
            )
        )
    for copy in loads:
        copy.start()
    roots_copy = pltpu.make_async_copy(roots_ref, roots_v, roots_sem)
    roots_copy.start()

    owners_copy.wait()
    lane = lax.broadcasted_iota(jnp.int32, (8, 128), 1)
    first = jnp.full((8, 128), -1, jnp.int32)
    last = jnp.full((8, 128), -1, jnp.int32)
    for k in range(total):
        last = jnp.where(lane == owners[k], k, last)
        first = jnp.where(lane == owners[total - 1 - k], total - 1 - k, first)
    table_v[0] = first
    table_v[1] = jnp.where(first == last, -1, last)
    table_copy = pltpu.make_async_copy(table_v, table, table_sem)
    table_copy.start()
    table_copy.wait()
    for copy in loads:
        copy.wait()

    mine = pl.ds(pl.multiple_of(me * rows, rows), rows)

    def pack(m, d):
        packed[m, d] = gv[jnp.maximum(table[m, 0, d], 0)]

    for m in range(slots):
        pack(m, me)
        pltpu.make_async_copy(
            packed.at[m, me], blocks.at[m, mine, :], recv_sem.at[0, m]
        ).start()

    for stage, group in enumerate(groups):
        if stage == 0:
            pl.semaphore_wait(barrier, len(group))
        else:
            reach = 2 ** (stage - 1)
            signal(near_sem.at[stage - 1], device(reach, 0))
            signal(near_sem.at[stage - 1], device(chips - reach, 0))
            pl.semaphore_wait(near_sem.at[stage - 1], 2)
        for m in range(slots):
            for step, other in group:
                to = device(step, other)
                pack(m, to)
                pltpu.make_async_remote_copy(
                    src_ref=packed.at[m, to],
                    dst_ref=blocks.at[m, mine, :],
                    send_sem=send_sem.at[0, m],
                    recv_sem=recv_sem.at[0, m],
                    device_id={"fsdp": to},
                    device_id_type=MESH,
                ).start()

    roots_copy.wait()
    backward = [partner for group in groups for partner in group][::-1]
    for m in range(slots):
        pltpu.make_async_copy(blocks.at[m], blocks.at[m], recv_sem.at[0, m]).wait()
        block = blocks[m]
        product = jnp.dot(
            block, roots_v[m, 1], preferred_element_type=jnp.float32
        ).astype(jnp.bfloat16)
        outgoing[m] = jnp.dot(
            roots_v[m, 0], product, preferred_element_type=jnp.float32
        ).astype(jnp.bfloat16)
        for step, other in backward:
            to = device(step, other)
            pltpu.make_async_remote_copy(
                src_ref=outgoing.at[m, pl.ds(pl.multiple_of(to * rows, rows), rows), :],
                dst_ref=returned.at[m, me],
                send_sem=send_sem.at[1, m],
                recv_sem=recv_sem.at[1, m],
                device_id={"fsdp": to},
                device_id_type=MESH,
            ).start()
        pltpu.make_async_copy(
            outgoing.at[m, mine, :], returned.at[m, me], recv_sem.at[1, m]
        ).start()
        kept = jnp.where(table[m, 0, me] >= 0, block, jnp.zeros_like(block))
        grams_v[m, 0] = lax.dot_general(
            kept, kept, (((1,), (1,)), ((), ())), preferred_element_type=jnp.float32
        ).astype(jnp.bfloat16)
        grams_v[m, 1] = lax.dot_general(
            kept, kept, (((0,), (0,)), ((), ())), preferred_element_type=jnp.float32
        ).astype(jnp.bfloat16)

    others = pl.ds(0, devices - 1)
    for m in range(slots):
        pltpu.make_async_copy(
            packed.at[m, others], packed.at[m, others], send_sem.at[0, m]
        ).wait()
    for m in range(slots):
        pltpu.make_async_copy(
            packed.at[m, others], packed.at[m, others], send_sem.at[1, m]
        ).wait()
        pltpu.make_async_copy(
            returned.at[m], returned.at[m], recv_sem.at[1, m]
        ).wait()
    for k in range(total):
        s, j = divmod(k, ncol)
        owner = owners[k]
        slot = jnp.where(table[0, 0, owner] == k, 0, 1)
        dir_v[s, :, j * order : (j + 1) * order] = returned[slot, owner]


def store(dir_in, grams_in, dir_ref, grams_ref, sems):
    copies = [
        pltpu.make_async_copy(grams_in, grams_ref, sems.at[0]),
        pltpu.make_async_copy(dir_in, dir_ref, sems.at[1]),
    ]
    for copy in copies:
        copy.start()
    for copy in copies:
        copy.wait()


def local(owners, grads, roots):
    devices = lax.axis_size("fsdp")
    slabs, rows, columns = grads.shape
    slots, _, order, _ = roots.shape
    ncol = columns // order
    total = slabs * ncol
    sizes = (devices, slabs, ncol, rows, order, slots)
    hbm = pl.BlockSpec(memory_space=pltpu.HBM)
    vmem = pl.BlockSpec(memory_space=pltpu.VMEM)
    bf16 = jnp.bfloat16
    stages = len(rings(devices // 2))
    owners, grads, roots = (
        pltpu.with_memory_space_constraint(x, pltpu.HBM) for x in (owners, grads, roots)
    )
    direction, grams = pl.pallas_call(
        functools.partial(exchange, sizes),
        out_shape=(pltpu.VMEM(grads.shape, bf16), pltpu.VMEM(roots.shape, bf16)),
        in_specs=[hbm, hbm, hbm],
        out_specs=(vmem, vmem),
        scratch_shapes=[
            pltpu.VMEM((total, rows, order), bf16),
            pltpu.VMEM((slots, devices, rows, order), bf16),
            pltpu.VMEM((slots, order, order), bf16),
            pltpu.VMEM(roots.shape, bf16),
            pltpu.VMEM((slots, order, order), bf16),
            pltpu.VMEM((slots, devices, rows, order), bf16),
            pltpu.VMEM((2, 8, 128), jnp.int32),
            pltpu.SMEM((2, 8, 128), jnp.int32),
            pltpu.SMEM((total,), jnp.int32),
            pltpu.SemaphoreType.DMA((total,)),
            pltpu.SemaphoreType.DMA,
            pltpu.SemaphoreType.DMA,
            pltpu.SemaphoreType.REGULAR((stages - 1,)),
            pltpu.SemaphoreType.DMA((2, slots)),
            pltpu.SemaphoreType.DMA((2, slots)),
        ],
        compiler_params=pltpu.CompilerParams(
            collective_id=0, has_side_effects=True, vmem_limit_bytes=32 << 20
        ),
        cost_estimate=pl.CostEstimate(
            flops=slots * 4 * 2 * order**3, bytes_accessed=6 << 20, transcendentals=0
        ),
    )(owners, grads, roots)
    return pl.pallas_call(
        store,
        out_shape=(
            jax.ShapeDtypeStruct(grads.shape, bf16),
            jax.ShapeDtypeStruct(roots.shape, bf16),
        ),
        in_specs=[vmem, vmem],
        out_specs=(hbm, hbm),
        scratch_shapes=[pltpu.SemaphoreType.DMA((2,))],
        compiler_params=pltpu.CompilerParams(vmem_limit_bytes=16 << 20),
    )(direction, grams)


def solution(mesh):
    return jax.shard_map(
        local,
        mesh=mesh,
        in_specs=(P("dp"), P("dp", "fsdp", None), P(("dp", "fsdp"), None, None, None)),
        out_specs=(P("dp", "fsdp", None), P(("dp", "fsdp"), None, None, None)),
        check_vma=False,
    )
```

```python
import functools

import jax
import jax.numpy as jnp
from jax import lax
from jax.experimental import pallas as pl
from jax.experimental.pallas import tpu as pltpu
from jax.sharding import PartitionSpec as P

MESH = pl.DeviceIdType.MESH
FIRST = 8


def rings(chips):
    groups, near, far = [], 0, 1
    while near < chips // 2:
        group = [(0, 1)] if near == 0 else []
        for distance in range(near + 1, min(far, chips // 2) + 1):
            for step in sorted({distance, chips - distance}):
                group += [(step, 0), (step, 1)]
        groups.append(group)
        near, far = far, 2 * far
    return groups


def exchange(
    sizes, owners_ref, grads_ref, roots_ref, returned, grams_v, spots,
    pieces, packed, blocks, roots_v, outgoing, table_v, table, owners,
    load_sem, table_sem, roots_sem, near_sem, send_sem, recv_sem,
):
    devices, slabs, ncol, rows, order, slots = sizes
    total = slabs * ncol
    chips = devices // 2
    me = lax.axis_index("fsdp")
    z, core = me // 2, lax.rem(me, 2)
    groups = rings(chips)

    def device(step, other):
        return lax.rem(z + step, chips) * 2 + lax.rem(core + other, 2)

    def signal(semaphore, to):
        pl.semaphore_signal(
            semaphore, inc=1, device_id={"fsdp": to}, device_id_type=MESH
        )

    owners_copy = pltpu.make_async_copy(owners_ref, owners, table_sem)
    owners_copy.start()
    barrier = pltpu.get_barrier_semaphore()
    for step, other in groups[0]:
        signal(barrier, device(step, other))
    loads = []
    for k in range(total):
        s, j = divmod(k, ncol)
        loads.append(
            pltpu.make_async_copy(
                grads_ref.at[s, :, pl.ds(j * order, order)], pieces.at[k], load_sem.at[k]
            )
        )
    for copy in loads:
        copy.start()
    roots_copy = pltpu.make_async_copy(roots_ref, roots_v, roots_sem)
    roots_copy.start()

    owners_copy.wait()
    lane = lax.broadcasted_iota(jnp.int32, (8, 128), 1)
    first = jnp.full((8, 128), -1, jnp.int32)
    last = jnp.full((8, 128), -1, jnp.int32)
    for k in range(total):
        last = jnp.where(lane == owners[k], k, last)
        first = jnp.where(lane == owners[total - 1 - k], total - 1 - k, first)
    table_v[0] = first
    table_v[1] = jnp.where(first == last, -1, last)
    table_copy = pltpu.make_async_copy(table_v, table, table_sem)
    table_copy.start()
    table_copy.wait()
    for copy in loads:
        copy.wait()

    mine = pl.ds(pl.multiple_of(me * rows, rows), rows)

    def pack(m, d):
        packed[m, d] = pieces[jnp.maximum(table[m, 0, d], 0)]

    for stage, group in enumerate(groups):
        if stage == 0:
            pl.semaphore_wait(barrier, len(group))
        else:
            reach = 2 ** (stage - 1)
            signal(near_sem.at[stage - 1], device(reach, 0))
            signal(near_sem.at[stage - 1], device(chips - reach, 0))
            pl.semaphore_wait(near_sem.at[stage - 1], 2)
        for m in range(slots):
            for step, other in group:
                to = device(step, other)
                pack(m, to)
                pltpu.make_async_remote_copy(
                    src_ref=packed.at[m, to],
                    dst_ref=blocks.at[m, mine, :],
                    send_sem=send_sem.at[0, m],
                    recv_sem=recv_sem.at[0, m],
                    device_id={"fsdp": to},
                    device_id_type=MESH,
                ).start()

    for m in range(slots):
        pack(m, me)
        pltpu.make_async_copy(
            packed.at[m, me], blocks.at[m, mine, :], recv_sem.at[0, m]
        ).start()
    for k in range(total):
        owner = owners[k]
        spots[k] = jnp.where(table[0, 0, owner] == k, owner, owner + devices)

    roots_copy.wait()
    for m in range(slots):
        pltpu.make_async_copy(blocks.at[m], blocks.at[m], recv_sem.at[0, m]).wait()
        block = blocks[m]
        product = jnp.dot(
            block, roots_v[m, 1], preferred_element_type=jnp.float32
        ).astype(jnp.bfloat16)
        outgoing[m] = jnp.dot(
            roots_v[m, 0], product, preferred_element_type=jnp.float32
        ).astype(jnp.bfloat16)

        def give(to, m=m):
            pltpu.make_async_remote_copy(
                src_ref=outgoing.at[m, pl.ds(pl.multiple_of(to * rows, rows), rows), :],
                dst_ref=returned.at[m * devices + me],
                send_sem=send_sem.at[1, m],
                recv_sem=recv_sem.at[1, m],
                device_id={"fsdp": to},
                device_id_type=MESH,
            ).start()

        early = FIRST if m == slots - 1 else 0
        for chip in range(early):

            @pl.when(chip != z)
            def _(chip=chip):
                give(chip * 2 + core)
                give(chip * 2 + 1 - core)

        for distance in range(chips // 2, 0, -1):
            for step in sorted({distance, chips - distance}):
                chip = lax.rem(z + step, chips)

                @pl.when(chip >= early)
                def _(chip=chip):
                    give(chip * 2 + core)
                    give(chip * 2 + 1 - core)

        give(device(0, 1))
        pltpu.make_async_copy(
            outgoing.at[m, mine, :], returned.at[m * devices + me], recv_sem.at[1, m]
        ).start()
        kept = jnp.where(table[m, 0, me] >= 0, block, jnp.zeros_like(block))
        grams_v[m, 0] = lax.dot_general(
            kept, kept, (((1,), (1,)), ((), ())), preferred_element_type=jnp.float32
        ).astype(jnp.bfloat16)
        grams_v[m, 1] = lax.dot_general(
            kept, kept, (((0,), (0,)), ((), ())), preferred_element_type=jnp.float32
        ).astype(jnp.bfloat16)

    others = pl.ds(0, devices - 1)
    for phase in range(2):
        for m in range(slots):
            pltpu.make_async_copy(
                packed.at[m, others], packed.at[m, others], send_sem.at[phase, m]
            ).wait()
            if phase == 1:
                part = pl.ds(m * devices, devices)
                pltpu.make_async_copy(
                    returned.at[part], returned.at[part], recv_sem.at[1, m]
                ).wait()


def store(sizes, spots, returned, grams_in, dir_ref, grams_ref, sems):
    devices, slabs, ncol, rows, order, slots = sizes
    total = slabs * ncol
    copies = [
        pltpu.make_async_copy(
            grams_in.at[m, i], grams_ref.at[m, i], sems.at[total + 2 * m + i]
        )
        for m in range(slots)
        for i in range(2)
    ]
    for k in range(total):
        s, j = divmod(k, ncol)
        copies.append(
            pltpu.make_async_copy(
                returned.at[spots[k]],
                dir_ref.at[s, :, pl.ds(j * order, order)],
                sems.at[k],
            )
        )
    for copy in copies:
        copy.start()
    for copy in copies:
        copy.wait()


def local(owners, grads, roots):
    devices = lax.axis_size("fsdp")
    slabs, rows, columns = grads.shape
    slots, _, order, _ = roots.shape
    ncol = columns // order
    total = slabs * ncol
    sizes = (devices, slabs, ncol, rows, order, slots)
    hbm = pl.BlockSpec(memory_space=pltpu.HBM)
    vmem = pl.BlockSpec(memory_space=pltpu.VMEM)
    smem = pl.BlockSpec(memory_space=pltpu.SMEM)
    bf16 = jnp.bfloat16
    stages = len(rings(devices // 2))
    owners, grads, roots = (
        pltpu.with_memory_space_constraint(x, pltpu.HBM) for x in (owners, grads, roots)
    )
    returned, grams, spots = pl.pallas_call(
        functools.partial(exchange, sizes),
        out_shape=(
            pltpu.VMEM((slots * devices, rows, order), bf16),
            pltpu.VMEM(roots.shape, bf16),
            pltpu.SMEM((total,), jnp.int32),
        ),
        in_specs=[hbm, hbm, hbm],
        out_specs=(vmem, vmem, smem),
        scratch_shapes=[
            pltpu.VMEM((total, rows, order), bf16),
            pltpu.VMEM((slots, devices, rows, order), bf16),
            pltpu.VMEM((slots, order, order), bf16),
            pltpu.VMEM(roots.shape, bf16),
            pltpu.VMEM((slots, order, order), bf16),
            pltpu.VMEM((2, 8, 128), jnp.int32),
            pltpu.SMEM((2, 8, 128), jnp.int32),
            pltpu.SMEM((total,), jnp.int32),
            pltpu.SemaphoreType.DMA((total,)),
            pltpu.SemaphoreType.DMA,
            pltpu.SemaphoreType.DMA,
            pltpu.SemaphoreType.REGULAR((stages - 1,)),
            pltpu.SemaphoreType.DMA((2, slots)),
            pltpu.SemaphoreType.DMA((2, slots)),
        ],
        compiler_params=pltpu.CompilerParams(
            collective_id=0, has_side_effects=True, vmem_limit_bytes=32 << 20
        ),
        cost_estimate=pl.CostEstimate(
            flops=slots * 4 * 2 * order**3, bytes_accessed=6 << 20, transcendentals=0
        ),
    )(owners, grads, roots)
    return pl.pallas_call(
        functools.partial(store, sizes),
        out_shape=(
            jax.ShapeDtypeStruct(grads.shape, bf16),
            jax.ShapeDtypeStruct(roots.shape, bf16),
        ),
        in_specs=[smem, vmem, vmem],
        out_specs=(hbm, hbm),
        scratch_shapes=[pltpu.SemaphoreType.DMA((total + 2 * slots,))],
        compiler_params=pltpu.CompilerParams(vmem_limit_bytes=16 << 20),
    )(spots, returned, grams)


def solution(mesh):
    return jax.shard_map(
        local,
        mesh=mesh,
        in_specs=(P("dp"), P("dp", "fsdp", None), P(("dp", "fsdp"), None, None, None)),
        out_specs=(P("dp", "fsdp", None), P(("dp", "fsdp"), None, None, None)),
        check_vma=False,
    )
```

```python
import functools

import jax
import jax.numpy as jnp
from jax import lax
from jax.experimental import pallas as pl
from jax.experimental.pallas import tpu as pltpu
from jax.sharding import PartitionSpec as P

MESH = pl.DeviceIdType.MESH
FIRST = 8


def rings(chips):
    groups, near, far = [], 0, 1
    while near < chips // 2:
        group = [(0, 1)] if near == 0 else []
        for distance in range(near + 1, min(far, chips // 2) + 1):
            for step in sorted({distance, chips - distance}):
                group += [(step, 0), (step, 1)]
        groups.append(group)
        near, far = far, 2 * far
    return groups


def exchange(
    sizes, owners_ref, grads_ref, roots_ref, returned, grams_v, spots,
    pieces, packed, blocks, roots_v, outgoing, table_v, table, owners,
    load_sem, table_sem, roots_sem, near_sem, send_sem, recv_sem,
):
    devices, slabs, ncol, rows, order, slots = sizes
    total = slabs * ncol
    chips = devices // 2
    me = lax.axis_index("fsdp")
    z, core = me // 2, lax.rem(me, 2)
    groups = rings(chips)

    def device(step, other):
        return lax.rem(z + step, chips) * 2 + lax.rem(core + other, 2)

    def signal(semaphore, to):
        pl.semaphore_signal(
            semaphore, inc=1, device_id={"fsdp": to}, device_id_type=MESH
        )

    owners_copy = pltpu.make_async_copy(owners_ref, owners, table_sem)
    owners_copy.start()
    barrier = pltpu.get_barrier_semaphore()
    for step, other in groups[0]:
        signal(barrier, device(step, other))
    loads = []
    for k in range(total):
        s, j = divmod(k, ncol)
        loads.append(
            pltpu.make_async_copy(
                grads_ref.at[s, :, pl.ds(j * order, order)], pieces.at[k], load_sem.at[k]
            )
        )
    for copy in loads:
        copy.start()
    roots_copy = pltpu.make_async_copy(roots_ref, roots_v, roots_sem)
    roots_copy.start()

    owners_copy.wait()
    lane = lax.broadcasted_iota(jnp.int32, (8, 128), 1)
    first = jnp.full((8, 128), -1, jnp.int32)
    last = jnp.full((8, 128), -1, jnp.int32)
    for k in range(total):
        last = jnp.where(lane == owners[k], k, last)
        first = jnp.where(lane == owners[total - 1 - k], total - 1 - k, first)
    table_v[0] = first
    table_v[1] = jnp.where(first == last, -1, last)
    table_copy = pltpu.make_async_copy(table_v, table, table_sem)
    table_copy.start()
    table_copy.wait()
    for copy in loads:
        copy.wait()

    mine = pl.ds(pl.multiple_of(me * rows, rows), rows)

    def pack(m, d):
        packed[m, d] = pieces[jnp.maximum(table[m, 0, d], 0)]

    for stage, group in enumerate(groups):
        if stage == 0:
            pl.semaphore_wait(barrier, len(group))
        else:
            reach = 2 ** (stage - 1)
            signal(near_sem.at[stage - 1], device(reach, 0))
            signal(near_sem.at[stage - 1], device(chips - reach, 0))
            pl.semaphore_wait(near_sem.at[stage - 1], 2)
        for m in range(slots):
            for step, other in group:
                to = device(step, other)
                pack(m, to)
                pltpu.make_async_remote_copy(
                    src_ref=packed.at[m, to],
                    dst_ref=blocks.at[m, mine, :],
                    send_sem=send_sem.at[0, m],
                    recv_sem=recv_sem.at[0, m],
                    device_id={"fsdp": to},
                    device_id_type=MESH,
                ).start()

    for m in range(slots):
        pack(m, me)
        pltpu.make_async_copy(
            packed.at[m, me], blocks.at[m, mine, :], recv_sem.at[0, m]
        ).start()
    for k in range(total):
        owner = owners[k]
        spots[k] = jnp.where(table[0, 0, owner] == k, owner, owner + devices)

    roots_copy.wait()
    for m in range(slots):
        pltpu.make_async_copy(blocks.at[m], blocks.at[m], recv_sem.at[0, m]).wait()
        block = blocks[m]
        product = jnp.dot(
            block, roots_v[m, 1], preferred_element_type=jnp.float32
        ).astype(jnp.bfloat16)
        outgoing[m] = jnp.dot(
            roots_v[m, 0], product, preferred_element_type=jnp.float32
        ).astype(jnp.bfloat16)

        def give(to, m=m):
            pltpu.make_async_remote_copy(
                src_ref=outgoing.at[m, pl.ds(pl.multiple_of(to * rows, rows), rows), :],
                dst_ref=returned.at[m * devices + me],
                send_sem=send_sem.at[1, m],
                recv_sem=recv_sem.at[1, m],
                device_id={"fsdp": to},
                device_id_type=MESH,
            ).start()

        early = FIRST if m == slots - 1 else 0
        for chip in range(early):

            @pl.when(chip != z)
            def _(chip=chip):
                give(chip * 2 + core)
                give(chip * 2 + 1 - core)

        for distance in range(chips // 2, 0, -1):
            for step in sorted({distance, chips - distance}):
                chip = lax.rem(z + step, chips)

                @pl.when(chip >= early)
                def _(chip=chip):
                    give(chip * 2 + core)
                    give(chip * 2 + 1 - core)

        give(device(0, 1))
        pltpu.make_async_copy(
            outgoing.at[m, mine, :], returned.at[m * devices + me], recv_sem.at[1, m]
        ).start()
        kept = jnp.where(table[m, 0, me] >= 0, block, jnp.zeros_like(block))
        grams_v[m, 0] = lax.dot_general(
            kept, kept, (((1,), (1,)), ((), ())), preferred_element_type=jnp.float32
        ).astype(jnp.bfloat16)
        grams_v[m, 1] = lax.dot_general(
            kept, kept, (((0,), (0,)), ((), ())), preferred_element_type=jnp.float32
        ).astype(jnp.bfloat16)

    others = pl.ds(0, devices - 1)
    for phase in range(2):
        for m in range(slots):
            pltpu.make_async_copy(
                packed.at[m, others], packed.at[m, others], send_sem.at[phase, m]
            ).wait()
            if phase == 1:
                part = pl.ds(m * devices, devices)
                pltpu.make_async_copy(
                    returned.at[part], returned.at[part], recv_sem.at[1, m]
                ).wait()


def store(sizes, spots, returned, grams_in, dir_ref, grams_ref, dir_v, sems):
    devices, slabs, ncol, rows, order, slots = sizes
    copies = [
        pltpu.make_async_copy(grams_in.at[m, i], grams_ref.at[m, i], sems.at[2 * m + i])
        for m in range(slots)
        for i in range(2)
    ]
    for copy in copies:
        copy.start()
    for s in range(slabs):
        for j in range(ncol):
            dir_v[s, :, j * order : (j + 1) * order] = returned[spots[s * ncol + j]]
        copies.append(
            pltpu.make_async_copy(dir_v.at[s], dir_ref.at[s], sems.at[2 * slots + s])
        )
        copies[-1].start()
    for copy in copies:
        copy.wait()


def local(owners, grads, roots):
    devices = lax.axis_size("fsdp")
    slabs, rows, columns = grads.shape
    slots, _, order, _ = roots.shape
    ncol = columns // order
    total = slabs * ncol
    sizes = (devices, slabs, ncol, rows, order, slots)
    hbm = pl.BlockSpec(memory_space=pltpu.HBM)
    vmem = pl.BlockSpec(memory_space=pltpu.VMEM)
    smem = pl.BlockSpec(memory_space=pltpu.SMEM)
    bf16 = jnp.bfloat16
    stages = len(rings(devices // 2))
    owners, grads, roots = (
        pltpu.with_memory_space_constraint(x, pltpu.HBM) for x in (owners, grads, roots)
    )
    returned, grams, spots = pl.pallas_call(
        functools.partial(exchange, sizes),
        out_shape=(
            pltpu.VMEM((slots * devices, rows, order), bf16),
            pltpu.VMEM(roots.shape, bf16),
            pltpu.SMEM((total,), jnp.int32),
        ),
        in_specs=[hbm, hbm, hbm],
        out_specs=(vmem, vmem, smem),
        scratch_shapes=[
            pltpu.VMEM((total, rows, order), bf16),
            pltpu.VMEM((slots, devices, rows, order), bf16),
            pltpu.VMEM((slots, order, order), bf16),
            pltpu.VMEM(roots.shape, bf16),
            pltpu.VMEM((slots, order, order), bf16),
            pltpu.VMEM((2, 8, 128), jnp.int32),
            pltpu.SMEM((2, 8, 128), jnp.int32),
            pltpu.SMEM((total,), jnp.int32),
            pltpu.SemaphoreType.DMA((total,)),
            pltpu.SemaphoreType.DMA,
            pltpu.SemaphoreType.DMA,
            pltpu.SemaphoreType.REGULAR((stages - 1,)),
            pltpu.SemaphoreType.DMA((2, slots)),
            pltpu.SemaphoreType.DMA((2, slots)),
        ],
        compiler_params=pltpu.CompilerParams(
            collective_id=0, has_side_effects=True, vmem_limit_bytes=32 << 20
        ),
        cost_estimate=pl.CostEstimate(
            flops=slots * 4 * 2 * order**3, bytes_accessed=6 << 20, transcendentals=0
        ),
    )(owners, grads, roots)
    return pl.pallas_call(
        functools.partial(store, sizes),
        out_shape=(
            jax.ShapeDtypeStruct(grads.shape, bf16),
            jax.ShapeDtypeStruct(roots.shape, bf16),
        ),
        in_specs=[smem, vmem, vmem],
        out_specs=(hbm, hbm),
        scratch_shapes=[
            pltpu.VMEM(grads.shape, bf16),
            pltpu.SemaphoreType.DMA((2 * slots + slabs,)),
        ],
        compiler_params=pltpu.CompilerParams(vmem_limit_bytes=16 << 20),
    )(spots, returned, grams)


def solution(mesh):
    return jax.shard_map(
        local,
        mesh=mesh,
        in_specs=(P("dp"), P("dp", "fsdp", None), P(("dp", "fsdp"), None, None, None)),
        out_specs=(P("dp", "fsdp", None), P(("dp", "fsdp"), None, None, None)),
        check_vma=False,
    )
```
